256 devices in a mesh: dp: 4 (over z_hi), expert: 64 (over z_lo, y, x, core).
Axes of the slice: x: 4, y: 4, z: 8 (z_hi: 4, z_lo: 2; z = z_hi * 2 + z_lo), core: 2. Of those that a mesh axis runs over, the one named last changes fastest.
Arguments:
- tokens: bfloat16 [32768, 1024], P(('dp', 'expert')), may hold values from -6 to 6
- cotangent: bfloat16 [32768, 1024], P(('dp', 'expert')), may hold values from -6 to 6
- route: int32 [32768, 2], P(('dp', 'expert')), may hold values from 0 to 63, all different within a row
- gates: float32 [32768, 2], P(('dp', 'expert')), may hold values from 0.2 to 1
- w_up: bfloat16 [64, 1024, 4096], P('expert', None, 'dp'), may hold values from -0.1875 to 0.1875
- w_down: bfloat16 [64, 4096, 1024], P('expert', 'dp'), may hold values from -0.09375 to 0.09375
- moment: bfloat16 [64, 1024, 4096], P('expert', None, 'dp'), may hold values from -24 to 24
- second: bfloat16 [64, 1024, 4096], P('expert', None, 'dp'), may hold values from 4 to 400
Outputs:
- layer_out: bfloat16 [32768, 1024], P(('dp', 'expert'))
- token_grad: bfloat16 [32768, 1024], P(('dp', 'expert'))
- update: bfloat16 [64, 1024, 4096], P('expert', None, 'dp')
The draws below stay inside these ranges and needn't reach their ends.
Inputs may be any that keep to these rules, and one draw needn't show every extreme that they name: `route`: each row names two different experts; every expert is named by some row.
All inputs are finite; a program needn't handle non-finite values.
Results may differ from the reference program's by a relative error of at most 0.0063.
Values may be sent and summed in bfloat16 or wider, within the bound.
A program may use at most 128 MiB of HBM per device.

```python
import math
import jax
import jax.numpy as jnp
from jax import lax

D = 1024
FF = 4096
TOK_DEV = 128
EXPERTS = 64
CAP = 4
TOKENS = 32768
N_DP = 4
N_EXPERT = 64


def shard_levels(rng, extent, pieces, least, high):
    level, own = 1.0, jax.random.fold_in(rng, 6)
    for axis_at, shards_of in pieces:
        heights = jnp.exp(jax.random.uniform(jax.random.fold_in(own, axis_at), (shards_of,), jnp.float32, least / len(pieces), high / len(pieces)))
        level = level * jnp.repeat(heights, extent[axis_at] // shards_of).reshape([-1 if axis == axis_at else 1 for axis in range(len(extent))])
    return level


def distinct(rng, rows, number_of, top, lift):
    order = jax.random.permutation(jax.random.fold_in(rng, 1), number_of)
    favour = order
    for power in range(3):
        favour = favour * favour // number_of
    favour = favour * lift // number_of
    lots = jax.random.randint(jax.random.fold_in(rng, 2), (rows, number_of), 0, 4096) + favour
    holders = jax.random.permutation(jax.random.fold_in(rng, 3), rows)[jnp.arange(number_of) % rows]
    lots = jnp.where(jnp.arange(rows)[:, None] == holders[None, :], 1 << 14, lots)
    score = lots * number_of + jnp.arange(number_of)
    return lax.top_k(score.astype(jnp.int32), top)[1].astype(jnp.int32)


def bell_draw(stream_key, extent, deviation, reach, shards=(), kind=jnp.bfloat16):
    result = jax.random.normal(stream_key, extent, jnp.float32) * deviation
    if len(shards) > 0:
        result = shard_levels(stream_key, extent, shards, -0.22, 0.18) * result
    return jnp.clip(result, min=-reach, max=reach).astype(kind)


def setup_inputs(seed: int = 0) -> dict:
    seeds = jax.random.split(jax.random.key(seed), 9)
    tokens = bell_draw(seeds[0], (TOKENS, D), 1.0, 6.0, ((0, 256),))
    cotangent = bell_draw(seeds[1], (TOKENS, D), 1.0, 6.0, ((0, 256),))
    route = distinct(seeds[2], TOKENS, EXPERTS, 2, 512)
    gates = jnp.clip(0.2 + 0.8 * jax.random.uniform(seeds[3], (TOKENS, 2), jnp.float32) ** shard_levels(seeds[3], (TOKENS, 2), ((0, 256),), -0.2, 0.2), 0.2, 1.0)
    w_up = bell_draw(seeds[4], (EXPERTS, D, FF), D ** -0.5, 0.1875, ((0, 64), (2, 4)))
    w_down = bell_draw(seeds[5], (EXPERTS, FF, D), FF ** -0.5, 0.09375, ((0, 64), (1, 4)))
    moment = bell_draw(seeds[6], (EXPERTS, D, FF), 4.0, 24.0, ((0, 64), (2, 4)))
    second = jnp.clip(jnp.exp(math.log(400.0) - 4.6051702 * jax.random.uniform(seeds[7], (EXPERTS, D, FF), jnp.float32) ** shard_levels(seeds[7], (EXPERTS, D, FF), ((0, 64), (2, 4)), -0.2, 0.2)), 4.0, 400.0).astype(jnp.bfloat16)
    return dict(tokens=tokens, cotangent=cotangent, route=route, gates=gates, w_up=w_up, w_down=w_down, moment=moment, second=second)


beta_first = 0.9
beta_second = 0.999
first_fix = 1.0 - 0.9 ** 10
second_fix = 1.0 - 0.999 ** 10
adam_eps = 1e-08
inv_root_two = 1.0 / math.sqrt(2.0)
inv_root_tau = 1.0 / math.sqrt(2.0 * math.pi)

def gelu_parts(preact):
    normal_cdf = 0.5 * (1.0 + jax.scipy.special.erf(preact * inv_root_two))
    density = jnp.exp(-0.5 * preact * preact) * inv_root_tau
    return (preact * normal_cdf, normal_cdf + preact * density)

def slot_table(route, capacity, experts):
    flat_experts = jnp.concatenate([route[:, 0], route[:, 1]]).astype(jnp.int32)
    one_hot = (flat_experts[:, None] == jnp.arange(experts, dtype=jnp.int32)[None, :]).astype(jnp.int32)
    earlier = (jnp.cumsum(one_hot, axis=0) - one_hot).astype(jnp.int32)
    position = lax.optimization_barrier(jnp.sum(earlier * one_hot, axis=1)).astype(jnp.int32)
    is_kept = position < capacity
    slot_index = (flat_experts * capacity + jnp.minimum(position, capacity - 1)).astype(jnp.int32)
    return (slot_index, is_kept)

def adam_direction(weight_grad, moment, second):
    first_moment = beta_first * moment.astype(jnp.float32) + (1.0 - beta_first) * weight_grad
    square = beta_second * second.astype(jnp.float32) + (1.0 - beta_second) * weight_grad * weight_grad
    return (first_moment / first_fix / (jnp.sqrt(square / second_fix) + adam_eps)).astype(jnp.bfloat16)

def expert_step(packed_rows, up_proj, down_proj, moment, second):
    model_width = packed_rows.shape[1] // 2
    inputs = packed_rows[:, :model_width]
    grad_rows = packed_rows[:, model_width:]
    preact = jnp.dot(inputs, up_proj, preferred_element_type=jnp.float32)
    hidden_act, gelu_slope = gelu_parts(preact)
    hidden = hidden_act.astype(jnp.bfloat16)
    expert_out = jnp.dot(hidden, down_proj, preferred_element_type=jnp.float32).astype(jnp.bfloat16)
    hidden_grad = lax.dot_general(grad_rows, down_proj, (((1,), (1,)), ((), ())), preferred_element_type=jnp.float32)
    preact_grad = (hidden_grad * gelu_slope).astype(jnp.bfloat16)
    input_grad = lax.dot_general(preact_grad, up_proj, (((1,), (1,)), ((), ())), preferred_element_type=jnp.float32).astype(jnp.bfloat16)
    weight_grad = lax.dot_general(inputs, preact_grad, (((0,), (0,)), ((), ())), preferred_element_type=jnp.float32)
    return (jnp.concatenate([expert_out, input_grad], axis=1), adam_direction(weight_grad, moment, second))

def scaled_rows(token_block, cotangent_block, gate_block):
    cot_float = cotangent_block.astype(jnp.float32)
    scaled = jnp.concatenate([gate_block[:, 0:1] * cot_float, gate_block[:, 1:2] * cot_float], axis=0).astype(jnp.bfloat16)
    return jnp.concatenate([jnp.concatenate([token_block, token_block], axis=0), scaled], axis=1)

def reference(tokens, cotangent, route, gates, w_up, w_down, moment, second):
    sources = N_DP * N_EXPERT
    model_width = tokens.shape[1]

    def dispatch(token_block, cotangent_block, route_block, gate_block):
        slot_index, is_kept = slot_table(route_block, CAP, EXPERTS)
        packed_rows = scaled_rows(token_block, cotangent_block, gate_block)
        target = jnp.where(is_kept, slot_index, EXPERTS * CAP).astype(jnp.int32)
        buffer = jnp.zeros((EXPERTS * CAP, 2 * model_width), jnp.bfloat16)
        return buffer.at[target].set(packed_rows, mode='drop')
    buffers = jax.vmap(dispatch)(tokens.reshape(sources, TOK_DEV, model_width), cotangent.reshape(sources, TOK_DEV, model_width), route.reshape(sources, TOK_DEV, 2), gates.reshape(sources, TOK_DEV, 2))
    per_expert = buffers.reshape(sources, EXPERTS, CAP, 2 * model_width).transpose(1, 0, 2, 3).reshape(EXPERTS, sources * CAP, 2 * model_width)

    def one_expert(operands):
        return expert_step(*operands)
    results, update = lax.map(one_expert, (per_expert, w_up, w_down, moment, second))
    back = results.reshape(EXPERTS, sources, CAP, 2 * model_width).transpose(1, 0, 2, 3).reshape(sources, EXPERTS * CAP, 2 * model_width)

    def combine(buffer, route_block, gate_block):
        slot_index, is_kept = slot_table(route_block, CAP, EXPERTS)
        picked = jnp.where(is_kept[:, None], buffer[slot_index].astype(jnp.float32), 0.0)
        first_rows = picked[:TOK_DEV]
        second_rows = picked[TOK_DEV:]
        layer_block = gate_block[:, 0:1] * first_rows[:, :model_width] + gate_block[:, 1:2] * second_rows[:, :model_width]
        grad_block = first_rows[:, model_width:] + second_rows[:, model_width:]
        return (layer_block.astype(jnp.bfloat16), grad_block.astype(jnp.bfloat16))
    layer_out, token_grad = jax.vmap(combine)(back, route.reshape(sources, TOK_DEV, 2), gates.reshape(sources, TOK_DEV, 2))
    return (layer_out.reshape(-1, model_width), token_grad.reshape(-1, model_width), update)
```

```python
import functools
import math

import jax
import jax.numpy as jnp
from jax import lax
from jax.experimental import pallas as pl
from jax.experimental.pallas import tpu as pltpu
from jax.sharding import PartitionSpec as P

beta_first = 0.9
beta_second = 0.999
first_fix = 1.0 - 0.9**10
second_fix = 1.0 - 0.999**10
adam_eps = 1e-08
inv_root_two = 1.0 / math.sqrt(2.0)
inv_root_tau = 1.0 / math.sqrt(2.0 * math.pi)

MESH = pl.DeviceIdType.MESH
F32 = jnp.float32
BF16 = jnp.bfloat16

NZ, NY, NX, NC = 8, 4, 4, 2
PLANE = NY * NX * NC
CAP = 4
TOK = 128
D = 1024
HID = 1024
ROWS = 1024
W = 256
NT = D // W
NQ = 2 * NT
HALF = TOK // 2
BLK = 256

RING = (0, -1, 1, -2, 2, -3, 3, 4)


def ring_at(distance):
    distance = (distance + 3) % NZ - 3
    return RING.index(distance)


def plane_order():
    def load(offset):
        total = [0, 0, 0, 0]
        for axis, step in ((0, offset[1]), (1, offset[0])):
            if step in (1, 2):
                total[2 * axis] += 1
            if step in (3, 2):
                total[2 * axis + 1] += 1
        return total

    rest = [
        (dy, dx, dc)
        for dy in range(NY)
        for dx in range(NX)
        for dc in range(NC)
        if (dy, dx, dc) != (0, 0, 0)
    ]
    now, order = [0, 0, 0, 0], []
    while rest:
        sums = {o: [a + b for a, b in zip(now, load(o))] for o in rest}
        best = min(rest, key=lambda o: (max(sums[o]) - min(sums[o]), -sum(load(o))))
        rest.remove(best)
        now = sums[best]
        order.append(best)
    return order


ORDER = plane_order()
OTHERS = len(ORDER)


def contract_last(left, right):
    return lax.dot_general(left, right, (((1,), (1,)), ((), ())), preferred_element_type=F32)


def contract_first(left, right):
    return lax.dot_general(left, right, (((0,), (0,)), ((), ())), preferred_element_type=F32)


def matmul(left, right):
    return jnp.dot(left, right, preferred_element_type=F32)


def kernel(
    tokens,
    cotangent,
    route,
    gates,
    w_up,
    w_down,
    moment,
    second,
    layer_out,
    token_grad,
    update,
    ring,
    stage,
    inbox,
    outbox,
    back,
    slope,
    hidden,
    up,
    down,
    first_in,
    second_in,
    selector,
    pick,
    slot_gate,
    token_gate,
    meta,
    part,
    sum_send,
    sum_recv,
    load_sem,
    weight_sem,
    store_sem,
    meta_send,
    meta_recv,
    ring_send,
    ring_recv,
    out_send,
    out_recv,
    ret_send,
    ret_recv,
    own_sem,
    sum_ssem,
    sum_rsem,
):
    dp = lax.axis_index("dp")
    expert = lax.axis_index("expert")
    z = dp * 2 + expert // PLANE
    y = (expert // (NX * NC)) % NY
    x = (expert // NC) % NX
    c = expert % NC
    mine = expert % PLANE
    z_lo = z % 2

    def in_ring(distance):
        there = (z + distance + NZ) % NZ
        return (there // 2, (there % 2) * PLANE + mine)

    def in_plane(offset, sign):
        dy, dx, dc = offset
        there = (((y + sign * dy + NY) % NY) * NX + (x + sign * dx + NX) % NX) * NC
        return there + (c + dc) % NC

    def device(place):
        return (dp, z_lo * PLANE + place)

    def rows_of(place):
        return pl.ds(pl.multiple_of(place * 32, 32), 32)

    def load(q):
        source = tokens if q < NT else cotangent
        return pltpu.make_async_copy(
            source.at[:, pl.ds((q % NT) * W, W)], ring.at[q, pl.ds(0, TOK)], load_sem.at[q]
        )

    weight_copies = [
        pltpu.make_async_copy(source.at[0], target, weight_sem.at[i])
        for i, (source, target) in enumerate(
            ((w_up, up), (w_down, down), (moment, first_in), (second, second_in))
        )
    ]
    for q in range(NQ):
        load(q).start()
    weight_copies[0].start()
    weight_copies[1].start()

    barrier = pltpu.get_barrier_semaphore()
    for offset in ORDER:
        pl.semaphore_signal(
            barrier, inc=1, device_id=device(in_plane(offset, 1)), device_id_type=MESH
        )
    for distance in range(1, NZ):
        pl.semaphore_signal(barrier, inc=1, device_id=in_ring(distance), device_id_type=MESH)

    experts = lax.broadcasted_iota(jnp.int32, (2 * PLANE, TOK), 0)
    one_hot = jnp.concatenate(
        [jnp.where(experts == route[k : k + 1, :], 1.0, 0.0) for k in range(2)], axis=1
    )
    before = lax.broadcasted_iota(jnp.int32, (2 * TOK, 2 * TOK), 0) < lax.broadcasted_iota(
        jnp.int32, (2 * TOK, 2 * TOK), 1
    )
    earlier = matmul(one_hot.astype(BF16), jnp.where(before, 1.0, 0.0).astype(BF16))
    position = jnp.sum(earlier * one_hot, axis=0, keepdims=True)
    slots = [
        jnp.where(
            position[:, k * TOK : (k + 1) * TOK] < CAP,
            32.0 * route[k : k + 1, :].astype(F32) + position[:, k * TOK : (k + 1) * TOK],
            -1e6,
        )
        for k in range(2)
    ]
    meta[0] = jnp.concatenate(
        slots + [gates[0:1, :], gates[1:2, :], jnp.zeros((4, TOK), F32)], axis=0
    )
    pl.semaphore_wait(barrier, OTHERS + NZ - 1)

    def ring_copy(q, way, step):
        sign = 1 if way == 0 else -1
        source, target = ring_at(-sign * (step - 1)), ring_at(-sign * step)
        rows, first = (TOK, 0) if step < 4 else (HALF, way * HALF)
        return pltpu.make_async_remote_copy(
            src_ref=ring.at[q, pl.ds(source * TOK + first, rows)],
            dst_ref=ring.at[q, pl.ds(target * TOK + first, rows)],
            send_sem=ring_send.at[q],
            recv_sem=ring_recv.at[(q * 2 + way) * 4 + step - 1],
            device_id=in_ring(sign),
            device_id_type=MESH,
        )

    def gather_step(q, step):
        if step == 1:
            load(q).wait()
        for way in range(2):
            if step > 1:
                ring_copy(q, way, step - 1).wait_recv()
            if step < 5:
                ring_copy(q, way, step).start()

    def meta_copy(distance):
        return pltpu.make_async_remote_copy(
            src_ref=meta.at[0],
            dst_ref=meta.at[ring_at(-distance)],
            send_sem=meta_send,
            recv_sem=meta_recv,
            device_id=in_ring(distance),
            device_id_type=MESH,
        )

    def whole(ref, sem):
        return pltpu.make_async_copy(ref, ref, sem)

    def slot_row(value, at):
        return value + (CAP * at - 1024 * z_lo).astype(F32)

    def build_selector():
        whole(meta.at[pl.ds(1, NZ - 1)], meta_recv).wait()

        @pl.loop(0, ROWS // BLK)
        def _(block):
            first = pl.multiple_of(block * BLK, BLK)
            row = (lax.broadcasted_iota(jnp.int32, (BLK, TOK), 0) + first).astype(F32)
            total = jnp.zeros((BLK, TOK), F32)
            for at in range(NZ):
                hit_0 = row == slot_row(meta[at, 0:1, :], at)
                hit_1 = row == slot_row(meta[at, 1:2, :], at)
                gate = jnp.where(
                    hit_0, meta[at, 2:3, :], jnp.where(hit_1, meta[at, 3:4, :], 0.0)
                )
                selector[pl.ds(first, BLK), pl.ds(at * TOK, TOK)] = jnp.where(
                    hit_0 | hit_1, 1.0, 0.0
                ).astype(BF16)
                total += gate
            slot_gate[pl.ds(first, BLK), :] = jnp.sum(total, axis=1, keepdims=True)

    def build_pick():
        columns = jnp.transpose(
            jnp.concatenate([meta[at] for at in range(NZ)] + [jnp.zeros((64, TOK), F32)], axis=0)
        )
        for at in range(NZ):
            here = pl.ds(at * TOK, TOK)
            column = lax.broadcasted_iota(jnp.int32, (TOK, ROWS), 1).astype(F32)
            for k in range(2):
                slot = slot_row(columns[:, at * 8 + k : at * 8 + k + 1], at)
                pick[k, here, :] = jnp.where(column == slot, 1.0, 0.0).astype(BF16)
                token_gate[k, here, :] = columns[:, at * 8 + 2 + k : at * 8 + 3 + k]

    def out_copy(q, i, offset):
        there = in_plane(offset, 1)
        return pltpu.make_async_remote_copy(
            src_ref=stage.at[q, rows_of(there)],
            dst_ref=inbox.at[q, pl.ds(i * 32, 32)],
            send_sem=out_send.at[q],
            recv_sem=out_recv.at[q],
            device_id=device(there),
            device_id_type=MESH,
        )

    def out_own(q):
        return pltpu.make_async_copy(
            stage.at[q, rows_of(mine)], inbox.at[q, pl.ds(OTHERS * 32, 32)], own_sem.at[q]
        )

    def ret_copy(q, i, offset):
        there = in_plane(offset, -1)
        return pltpu.make_async_remote_copy(
            src_ref=outbox.at[q, pl.ds(i * 32, 32)],
            dst_ref=back.at[q, rows_of(mine)],
            send_sem=ret_send.at[q],
            recv_sem=ret_recv.at[q],
            device_id=device(there),
            device_id_type=MESH,
        )

    def ret_own(q):
        return pltpu.make_async_copy(
            outbox.at[q, pl.ds(OTHERS * 32, 32)], back.at[q, rows_of(mine)], own_sem.at[q]
        )

    def others(ref, q):
        return ref.at[q, pl.ds(0, OTHERS * 32)]

    def dispatch(q):
        @pl.loop(0, ROWS // BLK)
        def _(block):
            here = pl.ds(pl.multiple_of(block * BLK, BLK), BLK)
            rows = matmul(selector[here, :], ring[q])
            if q >= NT:
                rows = rows * slot_gate[here, :]
            stage[q, here, :] = rows.astype(BF16)

        for i, offset in enumerate(ORDER):
            out_copy(q, i, offset).start()
        out_own(q).start()

    def arrived(q):
        whole(others(inbox, q), out_recv.at[q]).wait()
        out_own(q).wait()

    def send_back(q):
        for i, offset in enumerate(ORDER):
            ret_copy(q, i, offset).start()
        ret_own(q).start()

    def returned(q):
        whole(others(back, q), ret_recv.at[q]).wait()
        ret_own(q).wait()

    def forward_rows(block):
        here = pl.ds(block * BLK, BLK)

        @pl.loop(0, HID // BLK)
        def _(column):
            there = pl.ds(pl.multiple_of(column * BLK, BLK), BLK)
            preact = jnp.zeros((BLK, BLK), F32)
            for q in range(NT):
                preact += matmul(inbox[q, here, :], up[pl.ds(q * W, W), there])
            normal_cdf = 0.5 * (1.0 + lax.erf(preact * inv_root_two))
            density = jnp.exp(-0.5 * preact * preact) * inv_root_tau
            hidden[here, there] = (preact * normal_cdf).astype(BF16)
            slope[here, there] = normal_cdf + preact * density

    def forward_part(q):
        @pl.loop(0, ROWS // BLK)
        def _(block):
            here = pl.ds(pl.multiple_of(block * BLK, BLK), BLK)
            outbox[q, here, :] = matmul(hidden[here, :], down[:, pl.ds(q * W, W)]).astype(BF16)

        send_back(q)

    def backward_rows(block):
        here = pl.ds(block * BLK, BLK)

        @pl.loop(0, HID // BLK)
        def _(column):
            there = pl.ds(pl.multiple_of(column * BLK, BLK), BLK)
            grad = jnp.zeros((BLK, BLK), F32)
            for q in range(NT):
                grad += contract_last(inbox[NT + q, here, :], down[there, pl.ds(q * W, W)])
            hidden[here, there] = (grad * slope[here, there]).astype(BF16)

    def backward_part(q):
        @pl.loop(0, ROWS // BLK)
        def _(block):
            here = pl.ds(pl.multiple_of(block * BLK, BLK), BLK)
            outbox[NT + q, here, :] = contract_last(
                hidden[here, :], up[pl.ds(q * W, W), :]
            ).astype(BF16)

        send_back(NT + q)

    def update_rows(q):
        here = pl.ds(q * W, W)

        @pl.loop(0, HID // BLK)
        def _(column):
            there = pl.ds(pl.multiple_of(column * BLK, BLK), BLK)
            grad = contract_first(inbox[q], hidden[:, there])
            first = beta_first * first_in[here, there].astype(F32) + (1.0 - beta_first) * grad
            square = (
                beta_second * second_in[here, there].astype(F32)
                + (1.0 - beta_second) * grad * grad
            )
            first_in[here, there] = (
                first / first_fix / (jnp.sqrt(square / second_fix) + adam_eps)
            ).astype(BF16)

        update_copy(q).start()

    def update_copy(q):
        here = pl.ds(q * W, W)
        return pltpu.make_async_copy(first_in.at[here], update.at[0, here], store_sem.at[q])

    def combine(q):
        @pl.loop(0, ROWS // BLK)
        def _(block):
            here = pl.ds(pl.multiple_of(block * BLK, BLK), BLK)
            if q < NT:
                part[q % 2, here, :] = token_gate[0, here, :] * matmul(
                    pick[0, here, :], back[q]
                ) + token_gate[1, here, :] * matmul(pick[1, here, :], back[q])
            else:
                both = pick[0, here, :] + pick[1, here, :]
                part[q % 2, here, :] = matmul(both, back[q])

    def sum_copy(q, way, step):
        rows, first = (TOK, 0) if step > 1 else (HALF, way * HALF)
        return pltpu.make_async_remote_copy(
            src_ref=sum_send.at[q, way, step - 1, pl.ds(first, rows)],
            dst_ref=sum_recv.at[q, way, step - 1, pl.ds(first, rows)],
            send_sem=sum_ssem.at[q],
            recv_sem=sum_rsem.at[(q * 2 + way) * 4 + step - 1],
            device_id=in_ring(1 if way == 0 else -1),
            device_id_type=MESH,
        )

    def reduce_step(q, step):
        def mine_for(distance, first, rows):
            return part[q % 2, pl.ds(ring_at(distance) * TOK + first, rows), :]

        def got(way, at, first, rows):
            return sum_recv[q, way, at - 1, pl.ds(first, rows), :].astype(F32)

        if step == 5:
            total = mine_for(0, 0, TOK)
            for way in range(2):
                sum_copy(q, way, 4).wait_recv()
                total += got(way, 4, 0, TOK)
            target = layer_out if q < NT else token_grad
            target[:, pl.ds((q % NT) * W, W)] = total.astype(BF16)
            return
        for way in range(2):
            sign = 1 if way == 0 else -1
            first, other = way * HALF, (1 - way) * HALF
            if step == 1:
                sum_send[q, way, 0, pl.ds(first, HALF), :] = mine_for(4, first, HALF).astype(BF16)
            else:
                sum_copy(q, way, step - 1).wait_recv()
                distance = sign * (5 - step)
                if step == 2:
                    sum_send[q, way, 1, pl.ds(first, HALF), :] = (
                        mine_for(distance, first, HALF) + got(way, 1, first, HALF)
                    ).astype(BF16)
                    sum_send[q, way, 1, pl.ds(other, HALF), :] = mine_for(
                        distance, other, HALF
                    ).astype(BF16)
                else:
                    sum_send[q, way, step - 1] = (
                        mine_for(distance, 0, TOK) + got(way, step - 1, 0, TOK)
                    ).astype(BF16)
            sum_copy(q, way, step).start()

    for distance in range(1, NZ):
        meta_copy(distance).start()

    def forward_block(block):
        if block == 0:
            weight_copies[0].wait()
            for q in range(NT):
                arrived(q)
        forward_rows(block)

    filler = {0: [build_selector], 2: [build_pick]}
    for block in range(ROWS // BLK):
        filler[2 * NT + 5 + block] = [functools.partial(forward_block, block)]
    last = 2 * (NQ - 1) + 4
    for tick in range(last + 1):
        for q in range(NQ):
            step = tick - 2 * q + 1
            if 1 <= step <= 5:
                gather_step(q, step)
                if step == 5:
                    dispatch(q)
        for work in filler.pop(tick, ()):
            work()
    for tick in sorted(filler):
        for work in filler[tick]:
            work()

    weight_copies[1].wait()
    weight_copies[2].start()
    weight_copies[3].start()
    for q in range(NT):
        forward_part(q)
    for q in range(NT):
        arrived(NT + q)
    for block in range(ROWS // BLK):
        backward_rows(block)
    for q in range(NT):
        backward_part(q)
    weight_copies[2].wait()
    weight_copies[3].wait()

    for tick in range(last + 1):
        for q in range(NQ):
            step = tick - 2 * q + 1
            if step == 1:
                returned(q)
                combine(q)
            if 1 <= step <= 5:
                reduce_step(q, step)
        if tick % 2 == 1 and tick // 2 < NT:
            update_rows(tick // 2)

    whole(meta.at[pl.ds(1, NZ - 1)], meta_send).wait()
    for q in range(NQ):
        whole(ring.at[q, pl.ds(0, 7 * TOK)], ring_send.at[q]).wait()
        whole(others(stage, q), out_send.at[q]).wait()
        whole(others(outbox, q), ret_send.at[q]).wait()
        whole(ring.at[q, pl.ds(0, 7 * TOK)], sum_ssem.at[q]).wait()
    for q in range(NT):
        update_copy(q).wait()


def shards(tokens, cotangent, route, gates, w_up, w_down, moment, second):
    vmem = pl.BlockSpec(memory_space=pltpu.VMEM)
    anywhere = pl.BlockSpec(memory_space=pl.ANY)
    dma = pltpu.SemaphoreType.DMA
    chunks = pltpu.VMEM((NQ, ROWS, W), BF16)
    return pl.pallas_call(
        kernel,
        out_shape=(
            jax.ShapeDtypeStruct((TOK, D), BF16),
            jax.ShapeDtypeStruct((TOK, D), BF16),
            jax.ShapeDtypeStruct((1, D, HID), BF16),
        ),
        in_specs=[anywhere, anywhere, vmem, vmem, anywhere, anywhere, anywhere, anywhere],
        out_specs=(vmem, vmem, anywhere),
        scratch_shapes=[
            chunks,
            chunks,
            chunks,
            chunks,
            chunks,
            pltpu.VMEM((ROWS, HID), F32),
            pltpu.VMEM((ROWS, HID), BF16),
            pltpu.VMEM((D, HID), BF16),
            pltpu.VMEM((HID, D), BF16),
            pltpu.VMEM((D, HID), BF16),
            pltpu.VMEM((D, HID), BF16),
            pltpu.VMEM((ROWS, ROWS), BF16),
            pltpu.VMEM((2, ROWS, ROWS), BF16),
            pltpu.VMEM((ROWS, 1), F32),
            pltpu.VMEM((2, ROWS, 1), F32),
            pltpu.VMEM((NZ, 8, TOK), F32),
            pltpu.VMEM((2, ROWS, W), F32),
            pltpu.VMEM((NQ, 2, 4, TOK, W), BF16),
            pltpu.VMEM((NQ, 2, 4, TOK, W), BF16),
            dma((NQ,)),
            dma((4,)),
            dma((NT,)),
            dma,
            dma,
            dma((NQ,)),
            dma((NQ * 8,)),
            dma((NQ,)),
            dma((NQ,)),
            dma((NQ,)),
            dma((NQ,)),
            dma((NQ,)),
            dma((NQ,)),
            dma((NQ * 8,)),
        ],
        compiler_params=pltpu.CompilerParams(
            collective_id=0, has_side_effects=True, vmem_limit_bytes=62 << 20
        ),
        cost_estimate=pl.CostEstimate(
            flops=20 * 1024**3, bytes_accessed=12 << 20, transcendentals=3 << 20
        ),
        name="moe_step",
    )(tokens, cotangent, route.T, gates.T, w_up, w_down, moment, second)


def solution(mesh):
    in_specs = (
        P(("dp", "expert"), None),
        P(("dp", "expert"), None),
        P(("dp", "expert"), None),
        P(("dp", "expert"), None),
        P("expert", None, "dp"),
        P("expert", "dp", None),
        P("expert", None, "dp"),
        P("expert", None, "dp"),
    )
    out_specs = (P(("dp", "expert"), None), P(("dp", "expert"), None), P("expert", None, "dp"))
    return jax.shard_map(shards, mesh=mesh, in_specs=in_specs, out_specs=out_specs, check_vma=False)
```

```python
import functools
import math

import jax
import jax.numpy as jnp
from jax import lax
from jax.experimental import pallas as pl
from jax.experimental.pallas import tpu as pltpu
from jax.sharding import PartitionSpec as P

beta_first = 0.9
beta_second = 0.999
first_fix = 1.0 - 0.9**10
second_fix = 1.0 - 0.999**10
adam_eps = 1e-08
inv_root_two = 1.0 / math.sqrt(2.0)
inv_root_tau = 1.0 / math.sqrt(2.0 * math.pi)

MESH = pl.DeviceIdType.MESH
F32 = jnp.float32
BF16 = jnp.bfloat16

NZ, NY, NX, NC = 8, 4, 4, 2
PLANE = NY * NX * NC
CAP = 4
TOK = 128
D = 1024
HID = 1024
ROWS = 1024
W = 256
NT = D // W
NQ = 2 * NT
HALF = TOK // 2
GROUP = ROWS // 2
BLK = 256
PARTS = 4

RING = (0, -1, 1, -2, 2, -3, 3, 4)


def ring_at(distance):
    distance = (distance + 3) % NZ - 3
    return RING.index(distance)


def plane_order():
    def load(offset):
        total = [0, 0, 0, 0]
        for axis, step in ((0, offset[1]), (1, offset[0])):
            if step in (1, 2):
                total[2 * axis] += 1
            if step in (3, 2):
                total[2 * axis + 1] += 1
        return total

    rest = [
        (dy, dx, dc)
        for dy in range(NY)
        for dx in range(NX)
        for dc in range(NC)
        if (dy, dx, dc) != (0, 0, 0)
    ]
    now, order = [0, 0, 0, 0], []
    while rest:
        sums = {o: [a + b for a, b in zip(now, load(o))] for o in rest}
        best = min(rest, key=lambda o: (max(sums[o]) - min(sums[o]), -sum(load(o))))
        rest.remove(best)
        now = sums[best]
        order.append(best)
    return order


ORDER = plane_order()
OTHERS = len(ORDER)


def contract_last(left, right):
    return lax.dot_general(left, right, (((1,), (1,)), ((), ())), preferred_element_type=F32)


def contract_first(left, right):
    return lax.dot_general(left, right, (((0,), (0,)), ((), ())), preferred_element_type=F32)


def matmul(left, right):
    return jnp.dot(left, right, preferred_element_type=F32)


def kernel(
    tokens,
    cotangent,
    route,
    gates,
    w_up,
    w_down,
    moment,
    second,
    layer_out,
    token_grad,
    update,
    ring,
    stage,
    inbox,
    outbox,
    back,
    slope,
    hidden,
    up,
    down,
    first_in,
    second_in,
    selector,
    pick,
    slot_gate,
    token_gate,
    meta,
    part,
    sum_send,
    sum_recv,
    load_sem,
    weight_sem,
    store_sem,
    meta_send,
    meta_recv,
    ring_send,
    ring_recv,
    out_send,
    out_recv,
    ret_send,
    ret_recv,
    own_sem,
    sum_ssem,
    sum_rsem,
):
    dp = lax.axis_index("dp")
    expert = lax.axis_index("expert")
    z = dp * 2 + expert // PLANE
    y = (expert // (NX * NC)) % NY
    x = (expert // NC) % NX
    c = expert % NC
    mine = expert % PLANE
    z_lo = z % 2

    def in_ring(distance):
        there = (z + distance + NZ) % NZ
        return (there // 2, (there % 2) * PLANE + mine)

    def in_plane(offset, sign):
        dy, dx, dc = offset
        there = (((y + sign * dy + NY) % NY) * NX + (x + sign * dx + NX) % NX) * NC
        return there + (c + dc) % NC

    def device(place):
        return (dp, z_lo * PLANE + place)

    def load(q):
        source = tokens if q < NT else cotangent
        return pltpu.make_async_copy(
            source.at[:, pl.ds((q % NT) * W, W)], ring.at[q, pl.ds(0, TOK)], load_sem.at[q]
        )

    weight_copies = [
        pltpu.make_async_copy(source.at[0], target, weight_sem.at[i])
        for i, (source, target) in enumerate(
            ((w_up, up), (w_down, down), (moment, first_in), (second, second_in))
        )
    ]
    for q in range(NQ):
        load(q).start()
    weight_copies[0].start()
    weight_copies[1].start()

    barrier = pltpu.get_barrier_semaphore()
    for offset in ORDER:
        pl.semaphore_signal(
            barrier, inc=1, device_id=device(in_plane(offset, 1)), device_id_type=MESH
        )
    for distance in range(1, NZ):
        pl.semaphore_signal(barrier, inc=1, device_id=in_ring(distance), device_id_type=MESH)

    experts = lax.broadcasted_iota(jnp.int32, (2 * PLANE, TOK), 0)
    one_hot = jnp.concatenate(
        [jnp.where(experts == route[k : k + 1, :], 1.0, 0.0) for k in range(2)], axis=1
    )
    before = lax.broadcasted_iota(jnp.int32, (2 * TOK, 2 * TOK), 0) < lax.broadcasted_iota(
        jnp.int32, (2 * TOK, 2 * TOK), 1
    )
    earlier = matmul(one_hot.astype(BF16), jnp.where(before, 1.0, 0.0).astype(BF16))
    position = jnp.sum(earlier * one_hot, axis=0, keepdims=True)
    slots = [
        jnp.where(
            position[:, k * TOK : (k + 1) * TOK] < CAP,
            16.0 * route[k : k + 1, :].astype(F32) + position[:, k * TOK : (k + 1) * TOK],
            -1e6,
        )
        for k in range(2)
    ]
    meta[0] = jnp.concatenate(
        slots + [gates[0:1, :], gates[1:2, :], jnp.zeros((4, TOK), F32)], axis=0
    )
    pl.semaphore_wait(barrier, OTHERS + NZ - 1)

    def ring_copy(q, way, step):
        sign = 1 if way == 0 else -1
        source, target = ring_at(-sign * (step - 1)), ring_at(-sign * step)
        rows, first = (TOK, 0) if step < 4 else (HALF, way * HALF)
        return pltpu.make_async_remote_copy(
            src_ref=ring.at[q, pl.ds(source * TOK + first, rows)],
            dst_ref=ring.at[q, pl.ds(target * TOK + first, rows)],
            send_sem=ring_send.at[q],
            recv_sem=ring_recv.at[(q * 2 + way) * 4 + step - 1],
            device_id=in_ring(sign),
            device_id_type=MESH,
        )

    def gather_step(q, step):
        if step == 1:
            load(q).wait()
        for way in range(2):
            if step > 1:
                ring_copy(q, way, step - 1).wait_recv()
            if step < 5:
                ring_copy(q, way, step).start()

    def meta_copy(distance):
        return pltpu.make_async_remote_copy(
            src_ref=meta.at[0],
            dst_ref=meta.at[ring_at(-distance)],
            send_sem=meta_send,
            recv_sem=meta_recv,
            device_id=in_ring(distance),
            device_id_type=MESH,
        )

    def whole(ref, sem):
        return pltpu.make_async_copy(ref, ref, sem)

    def slot_row(value, at):
        return value + (CAP * (at % 4) - GROUP * z_lo).astype(F32)

    def build_selector():
        whole(meta.at[pl.ds(1, NZ - 1)], meta_recv).wait()

        for half in range(2):

            @pl.loop(0, GROUP // BLK)
            def _(block):
                first = pl.multiple_of(block * BLK, BLK)
                here = pl.ds(pl.multiple_of(half * GROUP + block * BLK, BLK), BLK)
                row = (lax.broadcasted_iota(jnp.int32, (BLK, TOK), 0) + first).astype(F32)
                total = jnp.zeros((BLK, TOK), F32)
                for i in range(4):
                    at = half * 4 + i
                    hit_0 = row == slot_row(meta[at, 0:1, :], at)
                    hit_1 = row == slot_row(meta[at, 1:2, :], at)
                    selector[here, pl.ds(i * TOK, TOK)] = jnp.where(
                        hit_0 | hit_1, 1.0, 0.0
                    ).astype(BF16)
                    total += jnp.where(
                        hit_0, meta[at, 2:3, :], jnp.where(hit_1, meta[at, 3:4, :], 0.0)
                    )
                slot_gate[here, :] = jnp.sum(total, axis=1, keepdims=True)

    def build_pick():
        columns = jnp.transpose(
            jnp.concatenate([meta[at] for at in range(NZ)] + [jnp.zeros((64, TOK), F32)], axis=0)
        )
        for at in range(NZ):
            here = pl.ds(at * TOK, TOK)
            column = lax.broadcasted_iota(jnp.int32, (TOK, GROUP), 1).astype(F32)
            for k in range(2):
                slot = slot_row(columns[:, at * 8 + k : at * 8 + k + 1], at)
                pick[k, here, :] = jnp.where(column == slot, 1.0, 0.0).astype(BF16)
                token_gate[k, here, :] = columns[:, at * 8 + 2 + k : at * 8 + 3 + k]

    def slots_of(half, place):
        return pl.ds(pl.multiple_of(half * GROUP + place * 16, 16), 16)

    def out_copy(q, half, i, offset):
        there = in_plane(offset, 1)
        return pltpu.make_async_remote_copy(
            src_ref=stage.at[q, slots_of(half, there)],
            dst_ref=inbox.at[q, pl.ds(half * GROUP + i * 16, 16)],
            send_sem=out_send.at[q * 2 + half],
            recv_sem=out_recv.at[q * 2 + half],
            device_id=device(there),
            device_id_type=MESH,
        )

    def out_own(q, half):
        return pltpu.make_async_copy(
            stage.at[q, slots_of(half, mine)],
            inbox.at[q, pl.ds(half * GROUP + OTHERS * 16, 16)],
            own_sem.at[q * 2 + half],
        )

    def ret_copy(q, half, i, offset):
        there = in_plane(offset, -1)
        return pltpu.make_async_remote_copy(
            src_ref=outbox.at[q, pl.ds(half * GROUP + i * 16, 16)],
            dst_ref=back.at[q, slots_of(half, mine)],
            send_sem=ret_send.at[q * 2 + half],
            recv_sem=ret_recv.at[q * 2 + half],
            device_id=device(there),
            device_id_type=MESH,
        )

    def ret_own(q, half):
        return pltpu.make_async_copy(
            outbox.at[q, pl.ds(half * GROUP + OTHERS * 16, 16)],
            back.at[q, slots_of(half, mine)],
            own_sem.at[q * 2 + half],
        )

    def others(ref, q, half):
        return ref.at[q, pl.ds(half * GROUP, OTHERS * 16)]

    def dispatch(q, half):
        @pl.loop(0, GROUP // BLK)
        def _(block):
            here = pl.ds(pl.multiple_of(half * GROUP + block * BLK, BLK), BLK)
            rows = matmul(selector[here, :], ring[q, pl.ds(half * GROUP, GROUP), :])
            if q >= NT:
                rows = rows * slot_gate[here, :]
            stage[q, here, :] = rows.astype(BF16)

        for i, offset in enumerate(ORDER):
            out_copy(q, half, i, offset).start()
        out_own(q, half).start()

    def arrived(q):
        for half in range(2):
            whole(others(inbox, q, half), out_recv.at[q * 2 + half]).wait()
            out_own(q, half).wait()

    def send_back(q):
        for half in (1, 0):
            for i, offset in enumerate(ORDER):
                ret_copy(q, half, i, offset).start()
            ret_own(q, half).start()

    def returned(q, half):
        whole(others(back, q, half), ret_recv.at[q * 2 + half]).wait()
        ret_own(q, half).wait()

    def forward_rows(block):
        here = pl.ds(block * BLK, BLK)

        @pl.loop(0, HID // BLK)
        def _(column):
            there = pl.ds(pl.multiple_of(column * BLK, BLK), BLK)
            preact = jnp.zeros((BLK, BLK), F32)
            for q in range(NT):
                preact += matmul(inbox[q, here, :], up[pl.ds(q * W, W), there])
            normal_cdf = 0.5 * (1.0 + lax.erf(preact * inv_root_two))
            density = jnp.exp(-0.5 * preact * preact) * inv_root_tau
            hidden[here, there] = (preact * normal_cdf).astype(BF16)
            slope[here, there] = normal_cdf + preact * density

    def forward_part(q):
        @pl.loop(0, ROWS // BLK)
        def _(block):
            here = pl.ds(pl.multiple_of(block * BLK, BLK), BLK)
            outbox[q, here, :] = matmul(hidden[here, :], down[:, pl.ds(q * W, W)]).astype(BF16)

        send_back(q)

    def backward_rows(block):
        here = pl.ds(block * BLK, BLK)

        @pl.loop(0, HID // BLK)
        def _(column):
            there = pl.ds(pl.multiple_of(column * BLK, BLK), BLK)
            grad = jnp.zeros((BLK, BLK), F32)
            for q in range(NT):
                grad += contract_last(inbox[NT + q, here, :], down[there, pl.ds(q * W, W)])
            hidden[here, there] = (grad * slope[here, there]).astype(BF16)

    def backward_part(q):
        @pl.loop(0, ROWS // BLK)
        def _(block):
            here = pl.ds(pl.multiple_of(block * BLK, BLK), BLK)
            outbox[NT + q, here, :] = contract_last(
                hidden[here, :], up[pl.ds(q * W, W), :]
            ).astype(BF16)

        send_back(NT + q)

    def update_rows(q, half):
        here = pl.ds(q * W, W)

        @pl.loop(half * (HID // BLK // 2), (half + 1) * (HID // BLK // 2))
        def _(column):
            there = pl.ds(pl.multiple_of(column * BLK, BLK), BLK)
            grad = contract_first(inbox[q], hidden[:, there])
            first = beta_first * first_in[here, there].astype(F32) + (1.0 - beta_first) * grad
            square = (
                beta_second * second_in[here, there].astype(F32)
                + (1.0 - beta_second) * grad * grad
            )
            first_in[here, there] = (
                first / first_fix / (jnp.sqrt(square / second_fix) + adam_eps)
            ).astype(BF16)

        if half == 1:
            update_copy(q).start()

    def update_copy(q):
        here = pl.ds(q * W, W)
        return pltpu.make_async_copy(first_in.at[here], update.at[0, here], store_sem.at[q])

    def combine(q, half):
        rows = back.at[q, pl.ds(half * GROUP, GROUP)]

        @pl.loop(0, GROUP // BLK)
        def _(block):
            here = pl.ds(pl.multiple_of(half * GROUP + block * BLK, BLK), BLK)
            if q < NT:
                part[q % PARTS, here, :] = token_gate[0, here, :] * matmul(
                    pick[0, here, :], rows[...]
                ) + token_gate[1, here, :] * matmul(pick[1, here, :], rows[...])
            else:
                both = pick[0, here, :] + pick[1, here, :]
                part[q % PARTS, here, :] = matmul(both, rows[...])

    def sum_copy(q, way, step):
        rows, first = (TOK, 0) if step > 1 else (HALF, way * HALF)
        return pltpu.make_async_remote_copy(
            src_ref=sum_send.at[q, way, step - 1, pl.ds(first, rows)],
            dst_ref=sum_recv.at[q, way, step - 1, pl.ds(first, rows)],
            send_sem=sum_ssem.at[q],
            recv_sem=sum_rsem.at[(q * 2 + way) * 4 + step - 1],
            device_id=in_ring(1 if way == 0 else -1),
            device_id_type=MESH,
        )

    def reduce_step(q, step):
        def mine_for(distance, first, rows):
            return part[q % PARTS, pl.ds(ring_at(distance) * TOK + first, rows), :]

        def got(way, at, first, rows):
            return sum_recv[q, way, at - 1, pl.ds(first, rows), :].astype(F32)

        if step == 5:
            total = mine_for(0, 0, TOK)
            for way in range(2):
                sum_copy(q, way, 4).wait_recv()
                total += got(way, 4, 0, TOK)
            target = layer_out if q < NT else token_grad
            target[:, pl.ds((q % NT) * W, W)] = total.astype(BF16)
            return
        for way in range(2):
            sign = 1 if way == 0 else -1
            first, other = way * HALF, (1 - way) * HALF
            if step == 1:
                sum_send[q, way, 0, pl.ds(first, HALF), :] = mine_for(4, first, HALF).astype(BF16)
            else:
                sum_copy(q, way, step - 1).wait_recv()
                distance = sign * (5 - step)
                if step == 2:
                    sum_send[q, way, 1, pl.ds(first, HALF), :] = (
                        mine_for(distance, first, HALF) + got(way, 1, first, HALF)
                    ).astype(BF16)
                    sum_send[q, way, 1, pl.ds(other, HALF), :] = mine_for(
                        distance, other, HALF
                    ).astype(BF16)
                else:
                    sum_send[q, way, step - 1] = (
                        mine_for(distance, 0, TOK) + got(way, step - 1, 0, TOK)
                    ).astype(BF16)
            sum_copy(q, way, step).start()

    for distance in range(1, NZ):
        meta_copy(distance).start()

    def forward_block(block):
        if block == 0:
            weight_copies[0].wait()
            for q in range(NT):
                arrived(q)
        forward_rows(block)

    filler = {0: [build_selector]}
    for block in range(ROWS // BLK):
        filler[NT + 5 + block] = [functools.partial(forward_block, block)]
    last = NQ + 3
    for tick in range(last + 1):
        steps = [(q, tick - q + 1) for q in range(NQ) if 1 <= tick - q + 1 <= 5]
        for q, step in steps:
            gather_step(q, step)
        for q, step in steps:
            if step in (3, 5):
                dispatch(q, 0 if step == 3 else 1)
        for work in filler.pop(tick, ()):
            work()
    for tick in sorted(filler):
        for work in filler[tick]:
            work()

    weight_copies[1].wait()
    weight_copies[2].start()
    weight_copies[3].start()
    for q in range(NT):
        forward_part(q)
    build_pick()
    for q in range(NT):
        arrived(NT + q)
    for block in range(ROWS // BLK):
        backward_rows(block)
    for q in range(NT):
        backward_part(q)
    weight_copies[2].wait()
    weight_copies[3].wait()

    for tick in range(last + 1):
        for q in range(NQ):
            step = tick - q + 1
            if step == 1 or step == 3:
                half = 1 if step == 1 else 0
                returned(q, half)
                combine(q, half)
            if 1 <= step <= 5:
                reduce_step(q, step)
        if tick < 2 * NT:
            update_rows(tick // 2, tick % 2)

    whole(meta.at[pl.ds(1, NZ - 1)], meta_send).wait()
    for q in range(NQ):
        whole(ring.at[q, pl.ds(0, 7 * TOK)], ring_send.at[q]).wait()
        for half in range(2):
            whole(others(stage, q, half), out_send.at[q * 2 + half]).wait()
            whole(others(outbox, q, half), ret_send.at[q * 2 + half]).wait()
        whole(ring.at[q, pl.ds(0, 7 * TOK)], sum_ssem.at[q]).wait()
    for q in range(NT):
        update_copy(q).wait()


def shards(tokens, cotangent, route, gates, w_up, w_down, moment, second):
    vmem = pl.BlockSpec(memory_space=pltpu.VMEM)
    anywhere = pl.BlockSpec(memory_space=pl.ANY)
    dma = pltpu.SemaphoreType.DMA
    chunks = pltpu.VMEM((NQ, ROWS, W), BF16)
    return pl.pallas_call(
        kernel,
        out_shape=(
            jax.ShapeDtypeStruct((TOK, D), BF16),
            jax.ShapeDtypeStruct((TOK, D), BF16),
            jax.ShapeDtypeStruct((1, D, HID), BF16),
        ),
        in_specs=[anywhere, anywhere, vmem, vmem, anywhere, anywhere, anywhere, anywhere],
        out_specs=(vmem, vmem, anywhere),
        scratch_shapes=[
            chunks,
            chunks,
            chunks,
            chunks,
            chunks,
            pltpu.VMEM((ROWS, HID), F32),
            pltpu.VMEM((ROWS, HID), BF16),
            pltpu.VMEM((D, HID), BF16),
            pltpu.VMEM((HID, D), BF16),
            pltpu.VMEM((D, HID), BF16),
            pltpu.VMEM((D, HID), BF16),
            pltpu.VMEM((ROWS, GROUP), BF16),
            pltpu.VMEM((2, ROWS, GROUP), BF16),
            pltpu.VMEM((ROWS, 1), F32),
            pltpu.VMEM((2, ROWS, 1), F32),
            pltpu.VMEM((NZ, 8, TOK), F32),
            pltpu.VMEM((PARTS, ROWS, W), F32),
            pltpu.VMEM((NQ, 2, 4, TOK, W), BF16),
            pltpu.VMEM((NQ, 2, 4, TOK, W), BF16),
            dma((NQ,)),
            dma((4,)),
            dma((NT,)),
            dma,
            dma,
            dma((NQ,)),
            dma((NQ * 8,)),
            dma((NQ * 2,)),
            dma((NQ * 2,)),
            dma((NQ * 2,)),
            dma((NQ * 2,)),
            dma((NQ * 2,)),
            dma((NQ,)),
            dma((NQ * 8,)),
        ],
        compiler_params=pltpu.CompilerParams(
            collective_id=0, has_side_effects=True, vmem_limit_bytes=62 << 20
        ),
        cost_estimate=pl.CostEstimate(
            flops=20 * 1024**3, bytes_accessed=12 << 20, transcendentals=3 << 20
        ),
        name="moe_step",
    )(tokens, cotangent, route.T, gates.T, w_up, w_down, moment, second)


def solution(mesh):
    in_specs = (
        P(("dp", "expert"), None),
        P(("dp", "expert"), None),
        P(("dp", "expert"), None),
        P(("dp", "expert"), None),
        P("expert", None, "dp"),
        P("expert", "dp", None),
        P("expert", None, "dp"),
        P("expert", None, "dp"),
    )
    out_specs = (P(("dp", "expert"), None), P(("dp", "expert"), None), P("expert", None, "dp"))
    return jax.shard_map(shards, mesh=mesh, in_specs=in_specs, out_specs=out_specs, check_vma=False)
```

```python
import functools
import math

import jax
import jax.numpy as jnp
from jax import lax
from jax.experimental import pallas as pl
from jax.experimental.pallas import tpu as pltpu
from jax.sharding import PartitionSpec as P

beta_first = 0.9
beta_second = 0.999
first_fix = 1.0 - 0.9**10
second_fix = 1.0 - 0.999**10
adam_eps = 1e-08
inv_root_two = 1.0 / math.sqrt(2.0)
inv_root_tau = 1.0 / math.sqrt(2.0 * math.pi)

MESH = pl.DeviceIdType.MESH
F32 = jnp.float32
BF16 = jnp.bfloat16

NZ, NY, NX, NC = 8, 4, 4, 2
PLANE = NY * NX * NC
CAP = 4
TOK = 128
D = 1024
HID = 1024
ROWS = 1024
W = 256
NT = D // W
NQ = 2 * NT
HALF = TOK // 2
GROUP = ROWS // 2
BLK = 256
PARTS = 8

RING = (0, -1, 1, -2, 2, -3, 3, 4)


def ring_at(distance):
    distance = (distance + 3) % NZ - 3
    return RING.index(distance)


def plane_order():
    def load(offset):
        total = [0, 0, 0, 0]
        for axis, step in ((0, offset[1]), (1, offset[0])):
            if step in (1, 2):
                total[2 * axis] += 1
            if step in (3, 2):
                total[2 * axis + 1] += 1
        return total

    rest = [
        (dy, dx, dc)
        for dy in range(NY)
        for dx in range(NX)
        for dc in range(NC)
        if (dy, dx, dc) != (0, 0, 0)
    ]
    now, order = [0, 0, 0, 0], []
    while rest:
        sums = {o: [a + b for a, b in zip(now, load(o))] for o in rest}
        best = min(rest, key=lambda o: (max(sums[o]) - min(sums[o]), -sum(load(o))))
        rest.remove(best)
        now = sums[best]
        order.append(best)
    return order


ORDER = plane_order()
OTHERS = len(ORDER)


def contract_last(left, right):
    return lax.dot_general(left, right, (((1,), (1,)), ((), ())), preferred_element_type=F32)


def contract_first(left, right):
    return lax.dot_general(left, right, (((0,), (0,)), ((), ())), preferred_element_type=F32)


def matmul(left, right):
    return jnp.dot(left, right, preferred_element_type=F32)


def kernel(
    tokens,
    cotangent,
    route,
    gates,
    w_up,
    w_down,
    moment,
    second,
    result,
    update,
    ring,
    stage,
    inbox,
    outbox,
    back,
    slope,
    hidden,
    up,
    down,
    first_in,
    second_in,
    selector,
    pick,
    slot_gate,
    token_gate,
    meta,
    part,
    sum_send,
    sum_recv,
    load_sem,
    weight_sem,
    store_sem,
    meta_send,
    meta_recv,
    ring_send,
    ring_recv,
    out_send,
    out_recv,
    ret_send,
    ret_recv,
    own_sem,
    sum_ssem,
    sum_rsem,
):
    dp = lax.axis_index("dp")
    expert = lax.axis_index("expert")
    z = dp * 2 + expert // PLANE
    y = (expert // (NX * NC)) % NY
    x = (expert // NC) % NX
    c = expert % NC
    mine = expert % PLANE
    z_lo = z % 2

    def in_ring(distance):
        there = (z + distance + NZ) % NZ
        return (there // 2, (there % 2) * PLANE + mine)

    def in_plane(offset, sign):
        dy, dx, dc = offset
        there = (((y + sign * dy + NY) % NY) * NX + (x + sign * dx + NX) % NX) * NC
        return there + (c + dc) % NC

    def device(place):
        return (dp, z_lo * PLANE + place)

    def load(q):
        source = tokens if q < NT else cotangent
        return pltpu.make_async_copy(
            source.at[:, pl.ds((q % NT) * W, W)], ring.at[q, pl.ds(0, TOK)], load_sem.at[q]
        )

    weight_copies = [
        pltpu.make_async_copy(source.at[0], target, weight_sem.at[i])
        for i, (source, target) in enumerate(
            ((w_up, up), (w_down, down), (moment, first_in), (second, second_in))
        )
    ]
    for q in range(NQ):
        load(q).start()
    weight_copies[0].start()
    weight_copies[1].start()

    barrier = pltpu.get_barrier_semaphore()
    for offset in ORDER:
        pl.semaphore_signal(
            barrier, inc=1, device_id=device(in_plane(offset, 1)), device_id_type=MESH
        )
    for distance in range(1, NZ):
        pl.semaphore_signal(barrier, inc=1, device_id=in_ring(distance), device_id_type=MESH)

    experts = lax.broadcasted_iota(jnp.int32, (2 * PLANE, TOK), 0)
    one_hot = jnp.concatenate(
        [jnp.where(experts == route[k : k + 1, :], 1.0, 0.0) for k in range(2)], axis=1
    )
    before = lax.broadcasted_iota(jnp.int32, (2 * TOK, 2 * TOK), 0) < lax.broadcasted_iota(
        jnp.int32, (2 * TOK, 2 * TOK), 1
    )
    earlier = matmul(one_hot.astype(BF16), jnp.where(before, 1.0, 0.0).astype(BF16))
    position = jnp.sum(earlier * one_hot, axis=0, keepdims=True)
    slots = [
        jnp.where(
            position[:, k * TOK : (k + 1) * TOK] < CAP,
            16.0 * route[k : k + 1, :].astype(F32) + position[:, k * TOK : (k + 1) * TOK],
            -1e6,
        )
        for k in range(2)
    ]
    meta[0] = jnp.concatenate(
        slots + [gates[0:1, :], gates[1:2, :], jnp.zeros((4, TOK), F32)], axis=0
    )
    pl.semaphore_wait(barrier, OTHERS + NZ - 1)

    def ring_copy(q, way, step):
        sign = 1 if way == 0 else -1
        source, target = ring_at(-sign * (step - 1)), ring_at(-sign * step)
        rows, first = (TOK, 0) if step < 4 else (HALF, way * HALF)
        return pltpu.make_async_remote_copy(
            src_ref=ring.at[q, pl.ds(source * TOK + first, rows)],
            dst_ref=ring.at[q, pl.ds(target * TOK + first, rows)],
            send_sem=ring_send.at[q],
            recv_sem=ring_recv.at[(q * 2 + way) * 4 + step - 1],
            device_id=in_ring(sign),
            device_id_type=MESH,
        )

    def gather_step(q, step):
        if step == 1:
            load(q).wait()
        for way in range(2):
            if step > 1:
                ring_copy(q, way, step - 1).wait_recv()
            if step < 5:
                ring_copy(q, way, step).start()

    def meta_copy(distance):
        return pltpu.make_async_remote_copy(
            src_ref=meta.at[0],
            dst_ref=meta.at[ring_at(-distance)],
            send_sem=meta_send,
            recv_sem=meta_recv,
            device_id=in_ring(distance),
            device_id_type=MESH,
        )

    def whole(ref, sem):
        return pltpu.make_async_copy(ref, ref, sem)

    def slot_row(value, at):
        return value + (CAP * (at % 4) - GROUP * z_lo).astype(F32)

    def build_selector():
        whole(meta.at[pl.ds(1, NZ - 1)], meta_recv).wait()

        for half in range(2):

            @pl.loop(0, GROUP // BLK)
            def _(block):
                first = pl.multiple_of(block * BLK, BLK)
                here = pl.ds(pl.multiple_of(half * GROUP + block * BLK, BLK), BLK)
                row = (lax.broadcasted_iota(jnp.int32, (BLK, TOK), 0) + first).astype(F32)
                total = jnp.zeros((BLK, TOK), F32)
                for i in range(4):
                    at = half * 4 + i
                    hit_0 = row == slot_row(meta[at, 0:1, :], at)
                    hit_1 = row == slot_row(meta[at, 1:2, :], at)
                    selector[here, pl.ds(i * TOK, TOK)] = jnp.where(
                        hit_0 | hit_1, 1.0, 0.0
                    ).astype(BF16)
                    total += jnp.where(
                        hit_0, meta[at, 2:3, :], jnp.where(hit_1, meta[at, 3:4, :], 0.0)
                    )
                slot_gate[here, :] = jnp.sum(total, axis=1, keepdims=True)

    def build_pick():
        columns = jnp.transpose(
            jnp.concatenate([meta[at] for at in range(NZ)] + [jnp.zeros((64, TOK), F32)], axis=0)
        )
        for at in range(NZ):
            here = pl.ds(at * TOK, TOK)
            column = lax.broadcasted_iota(jnp.int32, (TOK, GROUP), 1).astype(F32)
            for k in range(2):
                slot = slot_row(columns[:, at * 8 + k : at * 8 + k + 1], at)
                pick[k, here, :] = jnp.where(column == slot, 1.0, 0.0).astype(BF16)
                token_gate[k, here, :] = columns[:, at * 8 + 2 + k : at * 8 + 3 + k]

    def slots_of(half, place):
        return pl.ds(pl.multiple_of(half * GROUP + place * 16, 16), 16)

    def out_copy(q, half, i, offset):
        there = in_plane(offset, 1)
        return pltpu.make_async_remote_copy(
            src_ref=stage.at[q, slots_of(half, there)],
            dst_ref=inbox.at[q, pl.ds(half * GROUP + i * 16, 16)],
            send_sem=out_send.at[q * 2 + half],
            recv_sem=out_recv.at[q * 2 + half],
            device_id=device(there),
            device_id_type=MESH,
        )

    def out_own(q, half):
        return pltpu.make_async_copy(
            stage.at[q, slots_of(half, mine)],
            inbox.at[q, pl.ds(half * GROUP + OTHERS * 16, 16)],
            own_sem.at[q * 2 + half],
        )

    def ret_copy(q, half, i, offset):
        there = in_plane(offset, -1)
        return pltpu.make_async_remote_copy(
            src_ref=outbox.at[q, pl.ds(half * GROUP + i * 16, 16)],
            dst_ref=back.at[q, slots_of(half, mine)],
            send_sem=ret_send.at[q * 2 + half],
            recv_sem=ret_recv.at[q * 2 + half],
            device_id=device(there),
            device_id_type=MESH,
        )

    def ret_own(q, half):
        return pltpu.make_async_copy(
            outbox.at[q, pl.ds(half * GROUP + OTHERS * 16, 16)],
            back.at[q, slots_of(half, mine)],
            own_sem.at[q * 2 + half],
        )

    def others(ref, q, half):
        return ref.at[q, pl.ds(half * GROUP, OTHERS * 16)]

    def dispatch(q, half):
        @pl.loop(0, GROUP // BLK)
        def _(block):
            here = pl.ds(pl.multiple_of(half * GROUP + block * BLK, BLK), BLK)
            rows = matmul(selector[here, :], ring[q, pl.ds(half * GROUP, GROUP), :])
            if q >= NT:
                rows = rows * slot_gate[here, :]
            stage[q, here, :] = rows.astype(BF16)

        for i, offset in enumerate(ORDER):
            out_copy(q, half, i, offset).start()
        out_own(q, half).start()

    def arrived(q):
        for half in range(2):
            whole(others(inbox, q, half), out_recv.at[q * 2 + half]).wait()
            out_own(q, half).wait()

    def send_back(q):
        for half in (1, 0):
            for i, offset in enumerate(ORDER):
                ret_copy(q, half, i, offset).start()
            ret_own(q, half).start()

    def returned(q, half):
        whole(others(back, q, half), ret_recv.at[q * 2 + half]).wait()
        ret_own(q, half).wait()

    def forward_rows(block):
        here = pl.ds(block * BLK, BLK)

        @pl.loop(0, HID // BLK)
        def _(column):
            there = pl.ds(pl.multiple_of(column * BLK, BLK), BLK)
            preact = jnp.zeros((BLK, BLK), F32)
            for q in range(NT):
                preact += matmul(inbox[q, here, :], up[pl.ds(q * W, W), there])
            normal_cdf = 0.5 * (1.0 + lax.erf(preact * inv_root_two))
            density = jnp.exp(-0.5 * preact * preact) * inv_root_tau
            hidden[here, there] = (preact * normal_cdf).astype(BF16)
            slope[here, there] = normal_cdf + preact * density

    def forward_part(q):
        @pl.loop(0, ROWS // BLK)
        def _(block):
            here = pl.ds(pl.multiple_of(block * BLK, BLK), BLK)
            outbox[q, here, :] = matmul(hidden[here, :], down[:, pl.ds(q * W, W)]).astype(BF16)

        send_back(q)

    def backward_rows(block):
        here = pl.ds(block * BLK, BLK)

        @pl.loop(0, HID // BLK)
        def _(column):
            there = pl.ds(pl.multiple_of(column * BLK, BLK), BLK)
            grad = jnp.zeros((BLK, BLK), F32)
            for q in range(NT):
                grad += contract_last(inbox[NT + q, here, :], down[there, pl.ds(q * W, W)])
            hidden[here, there] = (grad * slope[here, there]).astype(BF16)

    def backward_part(q):
        @pl.loop(0, ROWS // BLK)
        def _(block):
            here = pl.ds(pl.multiple_of(block * BLK, BLK), BLK)
            outbox[NT + q, here, :] = contract_last(
                hidden[here, :], up[pl.ds(q * W, W), :]
            ).astype(BF16)

        send_back(NT + q)

    def update_rows(q, half):
        here = pl.ds(q * W, W)

        @pl.loop(half * (HID // BLK // 2), (half + 1) * (HID // BLK // 2))
        def _(column):
            there = pl.ds(pl.multiple_of(column * BLK, BLK), BLK)
            grad = contract_first(inbox[q], hidden[:, there])
            first = beta_first * first_in[here, there].astype(F32) + (1.0 - beta_first) * grad
            square = (
                beta_second * second_in[here, there].astype(F32)
                + (1.0 - beta_second) * grad * grad
            )
            first_in[here, there] = (
                first / first_fix / (jnp.sqrt(square / second_fix) + adam_eps)
            ).astype(BF16)

        if half == 1:
            update_copy(q).start()

    def update_copy(q):
        here = pl.ds(q * W, W)
        return pltpu.make_async_copy(first_in.at[here], update.at[0, here], store_sem.at[q])

    def combine(q, half):
        rows = back.at[q, pl.ds(half * GROUP, GROUP)]

        @pl.loop(0, GROUP // BLK)
        def _(block):
            here = pl.ds(pl.multiple_of(half * GROUP + block * BLK, BLK), BLK)
            if q < NT:
                part[q % PARTS, here, :] = token_gate[0, here, :] * matmul(
                    pick[0, here, :], rows[...]
                ) + token_gate[1, here, :] * matmul(pick[1, here, :], rows[...])
            else:
                both = pick[0, here, :] + pick[1, here, :]
                part[q % PARTS, here, :] = matmul(both, rows[...])

    def sum_copy(q, way, step):
        rows, first = (TOK, 0) if step > 1 else (HALF, way * HALF)
        return pltpu.make_async_remote_copy(
            src_ref=sum_send.at[q, way, step - 1, pl.ds(first, rows)],
            dst_ref=sum_recv.at[q, way, step - 1, pl.ds(first, rows)],
            send_sem=sum_ssem.at[q],
            recv_sem=sum_rsem.at[(q * 2 + way) * 4 + step - 1],
            device_id=in_ring(1 if way == 0 else -1),
            device_id_type=MESH,
        )

    def reduce_step(q, step):
        def mine_for(distance, first, rows):
            return part[q % PARTS, pl.ds(ring_at(distance) * TOK + first, rows), :]

        def got(way, at, first, rows):
            return sum_recv[q, way, at - 1, pl.ds(first, rows), :].astype(F32)

        if step == 5:
            total = mine_for(0, 0, TOK)
            for way in range(2):
                sum_copy(q, way, 4).wait_recv()
                total += got(way, 4, 0, TOK)
            result[pl.ds(q // NT * TOK, TOK), pl.ds((q % NT) * W, W)] = total.astype(BF16)
            return
        for way in range(2):
            sign = 1 if way == 0 else -1
            first, other = way * HALF, (1 - way) * HALF
            if step == 1:
                sum_send[q, way, 0, pl.ds(first, HALF), :] = mine_for(4, first, HALF).astype(BF16)
            else:
                sum_copy(q, way, step - 1).wait_recv()
                distance = sign * (5 - step)
                if step == 2:
                    sum_send[q, way, 1, pl.ds(first, HALF), :] = (
                        mine_for(distance, first, HALF) + got(way, 1, first, HALF)
                    ).astype(BF16)
                    sum_send[q, way, 1, pl.ds(other, HALF), :] = mine_for(
                        distance, other, HALF
                    ).astype(BF16)
                else:
                    sum_send[q, way, step - 1] = (
                        mine_for(distance, 0, TOK) + got(way, step - 1, 0, TOK)
                    ).astype(BF16)
            sum_copy(q, way, step).start()

    for distance in range(1, NZ):
        meta_copy(distance).start()

    def forward_block(block):
        if block == 0:
            weight_copies[0].wait()
            for q in range(NT):
                arrived(q)
        forward_rows(block)

    filler = {0: [build_selector]}
    for block in range(ROWS // BLK):
        filler[NT + 5 + block] = [functools.partial(forward_block, block)]
    last = NQ + 3
    for tick in range(last + 1):
        steps = [(q, tick - q + 1) for q in range(NQ) if 1 <= tick - q + 1 <= 5]
        for q, step in steps:
            gather_step(q, step)
        for q, step in steps:
            if step in (3, 5):
                dispatch(q, 0 if step == 3 else 1)
        for work in filler.pop(tick, ()):
            work()
    for tick in sorted(filler):
        for work in filler[tick]:
            work()

    weight_copies[1].wait()
    weight_copies[2].start()
    weight_copies[3].start()
    for q in range(NT):
        forward_part(q)
    build_pick()
    for q in range(NT):
        arrived(NT + q)
    for block in range(ROWS // BLK):
        backward_rows(block)
    for q in range(NT):
        backward_part(q)
    weight_copies[2].wait()
    weight_copies[3].wait()

    begin = [0 if q < NT else q - 2 for q in range(NQ)]
    for tick in range(max(begin) + 5):
        for q in range(NQ):
            step = tick - begin[q] + 1
            if step == 1 or step == 3:
                half = 1 if step == 1 else 0
                returned(q, half)
                combine(q, half)
            if 1 <= step <= 5:
                reduce_step(q, step)
        if tick < 2 * NT:
            update_rows(tick // 2, tick % 2)

    whole(meta.at[pl.ds(1, NZ - 1)], meta_send).wait()
    for q in range(NQ):
        whole(ring.at[q, pl.ds(0, 7 * TOK)], ring_send.at[q]).wait()
        for half in range(2):
            whole(others(stage, q, half), out_send.at[q * 2 + half]).wait()
            whole(others(outbox, q, half), ret_send.at[q * 2 + half]).wait()
        whole(ring.at[q, pl.ds(0, 7 * TOK)], sum_ssem.at[q]).wait()
    for q in range(NT):
        update_copy(q).wait()


def shards(tokens, cotangent, route, gates, w_up, w_down, moment, second):
    vmem = pl.BlockSpec(memory_space=pltpu.VMEM)
    anywhere = pl.BlockSpec(memory_space=pl.ANY)
    dma = pltpu.SemaphoreType.DMA
    chunks = pltpu.VMEM((NQ, ROWS, W), BF16)
    result, update = pl.pallas_call(
        kernel,
        out_shape=(
            jax.ShapeDtypeStruct((2 * TOK, D), BF16),
            jax.ShapeDtypeStruct((1, D, HID), BF16),
        ),
        in_specs=[anywhere, anywhere, vmem, vmem, anywhere, anywhere, anywhere, anywhere],
        out_specs=(vmem, anywhere),
        scratch_shapes=[
            chunks,
            chunks,
            chunks,
            chunks,
            chunks,
            pltpu.VMEM((ROWS, HID), F32),
            pltpu.VMEM((ROWS, HID), BF16),
            pltpu.VMEM((D, HID), BF16),
            pltpu.VMEM((HID, D), BF16),
            pltpu.VMEM((D, HID), BF16),
            pltpu.VMEM((D, HID), BF16),
            pltpu.VMEM((ROWS, GROUP), BF16),
            pltpu.VMEM((2, ROWS, GROUP), BF16),
            pltpu.VMEM((ROWS, 1), F32),
            pltpu.VMEM((2, ROWS, 1), F32),
            pltpu.VMEM((NZ, 8, TOK), F32),
            pltpu.VMEM((PARTS, ROWS, W), F32),
            pltpu.VMEM((NQ, 2, 4, TOK, W), BF16),
            pltpu.VMEM((NQ, 2, 4, TOK, W), BF16),
            dma((NQ,)),
            dma((4,)),
            dma((NT,)),
            dma,
            dma,
            dma((NQ,)),
            dma((NQ * 8,)),
            dma((NQ * 2,)),
            dma((NQ * 2,)),
            dma((NQ * 2,)),
            dma((NQ * 2,)),
            dma((NQ * 2,)),
            dma((NQ,)),
            dma((NQ * 8,)),
        ],
        compiler_params=pltpu.CompilerParams(
            collective_id=0, has_side_effects=True, vmem_limit_bytes=62 << 20
        ),
        cost_estimate=pl.CostEstimate(
            flops=20 * 1024**3, bytes_accessed=12 << 20, transcendentals=3 << 20
        ),
        name="moe_step",
    )(tokens, cotangent, route.T, gates.T, w_up, w_down, moment, second)
    return (result[:TOK], result[TOK:], update)


def solution(mesh):
    in_specs = (
        P(("dp", "expert"), None),
        P(("dp", "expert"), None),
        P(("dp", "expert"), None),
        P(("dp", "expert"), None),
        P("expert", None, "dp"),
        P("expert", "dp", None),
        P("expert", None, "dp"),
        P("expert", None, "dp"),
    )
    out_specs = (P(("dp", "expert"), None), P(("dp", "expert"), None), P("expert", None, "dp"))
    return jax.shard_map(shards, mesh=mesh, in_specs=in_specs, out_specs=out_specs, check_vma=False)
```
